32 devices in a mesh: cases: 2 (over x), row: 8 (over z, y), col: 2 (over core).
Axes of the slice: x: 2, y: 2, z: 4, core: 2. Of those that a mesh axis runs over, the one named last changes fastest.
Arguments:
- markov_head: bfloat16 [32, 500, 500], P(('cases', 'row')), parts along dimension 0, may hold values from -0.0625 to 0.0625
- markov_tail: bfloat16 [32, 500, 500], P(('cases', 'col')), parts along dimension 0, may hold values from -0.0625 to 0.0625
- probes: bfloat16 [16000, 128], P(('cases', 'col')), parts along dimension 0, may hold values from -6 to 6
Outputs:
- sketch: float32 [16000, 128], P(('cases', 'row')), parts along dimension 0
- back_now: float32 [16000, 128], P(('cases', 'col')), parts along dimension 0
- back_next: float32 [16000, 128], P(('cases', 'col')), parts along dimension 0
The draws below stay inside these ranges and needn't reach their ends.
There are 2 independent parts, one for each index of `cases`. The reference program is written for one: setup_inputs(seed, part) draws one part's arguments, and reference() takes and returns one part's arrays. A program takes and returns all parts, laid end to end along the dimension named above; each array names one. Nothing has to cross between parts.
All inputs are finite; a program needn't handle non-finite values.
Results may differ from the reference program's by a relative error of at most 0.0022.
Values may be sent and summed in bfloat16 or wider, within the bound.
A program may use at most 128 MiB of HBM per device.

```python
import jax
import jax.numpy as jnp
from jax import lax

PORTS = 500
PROBES = 128
BLOCK_ROWS = 16
BLOCK_COLS = 16


def level_of(stream_key, extent, shards, least, top_value):
    gain, own = 1.0, jax.random.fold_in(stream_key, 6)
    for position, blocks in shards:
        heights = jnp.exp(jax.random.uniform(jax.random.fold_in(own, position), (blocks,), jnp.float32, least / len(shards), top_value / len(shards)))
        gain = gain * jnp.repeat(heights, extent[position] // blocks).reshape([-1 if axis == position else 1 for axis in range(len(extent))])
    return gain


def bell_draw(stream_key, extent, width, limit, pieces=(), kind=jnp.bfloat16):
    level = level_of(stream_key, extent, pieces, -0.22, 0.18) if pieces else 1.0
    values = jax.random.normal(stream_key, extent, jnp.float32) * width * level
    return jnp.minimum(jnp.maximum(values, -limit), limit).astype(kind)


def setup_inputs(seed: int = 0, part: int = 0) -> dict:
    seeds = jax.random.split(jax.random.key(seed), 4)
    own_keys = jax.random.split(jax.random.fold_in(seeds[3], part), 4)
    markov_head = bell_draw(own_keys[0], (BLOCK_ROWS, PORTS, PORTS), (16 * PORTS) ** -0.5, 0.0625, ((0, 8),))
    markov_tail = bell_draw(own_keys[1], (BLOCK_COLS, PORTS, PORTS), (16 * PORTS) ** -0.5, 0.0625, ((0, 2),))
    probes = bell_draw(own_keys[2], (BLOCK_COLS * PORTS, PROBES), 1.0, 6.0, ((0, 2),))
    return {"markov_head": markov_head, "markov_tail": markov_tail, "probes": probes}


def reference(markov_head, markov_tail, probes):
    markov = jnp.concatenate([markov_head, markov_tail], axis=0)
    blocks = probes.reshape(BLOCK_COLS, PORTS, PROBES).astype(jnp.float32)

    def row_pass(index):
        tiles = lax.dynamic_slice_in_dim(markov, index, BLOCK_COLS, 0).astype(jnp.float32)
        return jnp.einsum('jpq,jqk->pk', tiles, blocks)

    sketch = lax.map(row_pass, jnp.arange(BLOCK_ROWS, dtype=jnp.int32))
    rounded = lax.optimization_barrier(sketch.astype(jnp.bfloat16)).astype(jnp.float32)

    def col_pass(totals, inputs):
        index, block_row = inputs
        tiles = lax.dynamic_slice_in_dim(markov, index, BLOCK_COLS + 1, 0).astype(jnp.float32)
        current = totals[0] + jnp.einsum('jqp,qk->jpk', tiles[:BLOCK_COLS], block_row)
        shifted = totals[1] + jnp.einsum('jqp,qk->jpk', tiles[1:], block_row)
        return (current, shifted), None

    empty = jnp.zeros((BLOCK_COLS, PORTS, PROBES), jnp.float32)
    totals, unused = lax.scan(col_pass, (empty, empty), (jnp.arange(BLOCK_ROWS, dtype=jnp.int32), rounded))
    return (sketch.reshape(BLOCK_ROWS * PORTS, PROBES),
            totals[0].reshape(BLOCK_COLS * PORTS, PROBES),
            totals[1].reshape(BLOCK_COLS * PORTS, PROBES))
```

```python
import jax
import jax.numpy as jnp
from jax import lax
from jax.experimental import pallas as pl
from jax.experimental.pallas import tpu as pltpu
from jax.sharding import PartitionSpec as P

LANES = 128
MESH = pl.DeviceIdType.MESH


def spread(x, axis, root):
    mine = lax.axis_index(axis) == root
    return lax.psum(jnp.where(mine, x, jnp.zeros_like(x)), axis)


def from_behind(x, axis, by):
    peers = lax.axis_size(axis)
    pairs = [(i, i + by) for i in range(peers) if 0 <= i + by < peers]
    return lax.ppermute(x, axis, pairs)


def store_slot(window, target, shard):
    slot_count = window.shape[0]
    inside = (target >= 0) & (target < slot_count)
    placed = jnp.clip(target, 0, slot_count - 1)
    present = lax.dynamic_index_in_dim(window, placed, 0, keepdims=False)
    return lax.dynamic_update_index_in_dim(window, jnp.where(inside, shard, present), placed, 0)


def body(markov_head, markov_tail, probes):
    rows_held = markov_head.shape[0]
    order = markov_head.shape[1]
    cols_held = markov_tail.shape[0]
    columns = probes.shape[1]
    row_count = lax.axis_size("row")
    row_place = lax.axis_index("row")
    col_place = lax.axis_index("col")
    strides = cols_held // rows_held
    slot_count = strides + 1
    blocks = probes.reshape(cols_held, order, columns)
    leading = spread(markov_tail, "col", 0)
    full_tail = jnp.concatenate([leading, markov_tail], axis=0)
    window = jnp.zeros((slot_count, rows_held, order, order), markov_head.dtype)

    def march_turn(number, status):
        window_now, carried = status
        window_now = store_slot(window_now, number - col_place * strides, carried)
        carried = from_behind(carried, "row", -1)
        return (window_now, carried)

    window, carried = lax.fori_loop(0, 2 * strides, march_turn, (window, markov_head))
    window = store_slot(window, 2 * strides - col_place * strides, carried)
    shard_ids = row_place + col_place * strides + jnp.arange(slot_count, dtype=jnp.int32)
    offsets = jnp.clip((shard_ids - row_count) * rows_held, 0, 2 * cols_held - rows_held)

    def tail_piece(anchor):
        return lax.dynamic_slice_in_dim(full_tail, anchor, rows_held, 0)

    from_tail = jax.vmap(tail_piece)(offsets)
    window = jnp.where((shard_ids >= row_count)[:, None, None, None], from_tail, window)
    window = window.reshape(slot_count * rows_held, order, order)
    partial_rows = jnp.stack(
        [
            jnp.einsum(
                "jpq,jqk->pk",
                window[offset : offset + cols_held],
                blocks,
                preferred_element_type=jnp.float32,
            )
            for offset in range(rows_held)
        ]
    ).reshape(rows_held * order, columns)
    sketch = lax.psum(partial_rows, "col")
    rounded = sketch.astype(jnp.bfloat16).reshape(rows_held, order, columns)
    current_sum = jnp.zeros((cols_held, order, columns), jnp.float32)
    shifted_sum = jnp.zeros((cols_held, order, columns), jnp.float32)
    for offset in range(rows_held):
        current_sum = current_sum + jnp.einsum(
            "jqp,qk->jpk",
            window[offset : offset + cols_held],
            rounded[offset],
            preferred_element_type=jnp.float32,
        )
        shifted_sum = shifted_sum + jnp.einsum(
            "jqp,qk->jpk",
            window[offset + 1 : offset + 1 + cols_held],
            rounded[offset],
            preferred_element_type=jnp.float32,
        )
    back_now, back_next = lax.psum(
        (
            current_sum.reshape(cols_held * order, columns),
            shifted_sum.reshape(cols_held * order, columns),
        ),
        "row",
    )
    return (sketch, back_now, back_next)


def gathered_kernel(head_ref, tail_ref, probe_ref, sk_ref, y_ref, m, px, st, acc, yacc,
                    local_sem, zsend, ysend, ssend, piece_recv, sib_recv, xsend, xrecv):
    f32 = jnp.float32
    r = lax.axis_index("row")
    c = lax.axis_index("col")
    other = 1 - c
    z, y = r // 2, r % 2
    mate = r + 1 - 2 * y
    layers = lax.axis_size("row") // 2

    load_head = pltpu.make_async_copy(head_ref, m.at[pl.ds(2 * r, 2)], local_sem.at[0])
    load_probe = pltpu.make_async_copy(
        probe_ref, px.at[:, pl.ds(pl.multiple_of((9 - 8 * c) * LANES, LANES), 8 * LANES)], local_sem.at[1])
    load_tail = pltpu.make_async_copy(tail_ref, m.at[pl.ds(16 + 8 * c, 8)], local_sem.at[2])
    load_head.start()
    load_probe.start()
    load_tail.start()

    barrier = pltpu.get_barrier_semaphore()

    def greet(row, col):
        pl.semaphore_signal(barrier, inc=1, device_id={"row": row, "col": col}, device_id_type=MESH)

    greet(r, other)
    greet(mate, c)

    @pl.when(z > 0)
    def _():
        greet(r - 2, c)

    @pl.when(z < layers - 1)
    def _():
        greet(r + 2, c)

    zero_columns = jnp.zeros((px.shape[0], LANES), px.dtype)
    px[:, 0:LANES] = zero_columns
    px[:, 17 * LANES:18 * LANES] = zero_columns
    zero_rows = jnp.zeros((LANES, st.shape[1]), st.dtype)
    st[0:LANES, :] = zero_rows
    st[17 * LANES:18 * LANES, :] = zero_rows
    acc[...] = jnp.zeros_like(acc)
    pl.semaphore_wait(barrier, 2 + (z > 0).astype(jnp.int32) + (z < layers - 1).astype(jnp.int32))

    def along_z(s, up):
        return pltpu.make_async_remote_copy(
            m.at[2 * s + c], m.at[2 * s + c], zsend.at[up * 8 + s], piece_recv.at[s],
            device_id={"row": r + 4 * up - 2, "col": c}, device_id_type=MESH)

    def along_y(s):
        return pltpu.make_async_remote_copy(
            m.at[2 * s + c], m.at[2 * s + c], ysend.at[s], piece_recv.at[s],
            device_id={"row": mate, "col": c}, device_id_type=MESH)

    def to_core(s):
        return pltpu.make_async_remote_copy(
            m.at[2 * s + c], m.at[2 * s + c], ssend.at[s], sib_recv.at[s],
            device_id={"row": r, "col": other}, device_id_type=MESH)

    def from_core(s):
        return pltpu.make_async_remote_copy(
            m.at[2 * s + other], m.at[2 * s + other], ssend.at[s], sib_recv.at[s],
            device_id={"row": r, "col": other}, device_id_type=MESH)

    def swap(ref_of, slot):
        return pltpu.make_async_remote_copy(
            ref_of(c), ref_of(c), xsend.at[slot], xrecv.at[slot],
            device_id={"row": r, "col": other}, device_id_type=MESH)

    def swapped(ref_of, slot):
        return pltpu.make_async_remote_copy(
            ref_of(other), ref_of(other), xsend.at[slot], xrecv.at[slot],
            device_id={"row": r, "col": other}, device_id_type=MESH)

    def probe_part(core):
        return px.at[:, pl.ds(pl.multiple_of((9 - 8 * core) * LANES, LANES), 8 * LANES)]

    def tail_part(core):
        return m.at[pl.ds(16 + 8 * core, 8)]

    def sketch_part(core):
        return st.at[pl.ds(pl.multiple_of((9 - 8 * core) * LANES, LANES), 8 * LANES), :]

    load_head.wait()
    along_y(r).start()

    @pl.when(z > 0)
    def _():
        along_z(r, 0).start()

    @pl.when(z < layers - 1)
    def _():
        along_z(r, 1).start()

    load_probe.wait()
    swap(probe_part, 0).start()
    load_tail.wait()

    @pl.when(c == 0)
    def _():
        swap(tail_part, 1).start()

    def use(first, count):
        def turn(step, carry):
            k = first + step // 4
            g = step % 4
            lag = k - 8 * c - 2 * g

            @pl.when((lag >= 0) & (lag <= 16))
            def _():
                spot = pl.multiple_of((16 - lag) * LANES, LANES)
                acc[g] += jnp.dot(m[k], px[:, pl.ds(spot, 2 * LANES)], preferred_element_type=f32)

            return carry

        lax.fori_loop(0, 4 * count, turn, 0)

    def wanted(s, core):
        return (core == 0) | (s >= 4)

    def use_chip(s):
        @pl.when(wanted(s, c))
        def _():
            from_core(s).wait_recv()
            use(2 * s, 2)

    def each_side(base, distance, act):
        for up in (0, 1):
            there = z + distance * (2 * up - 1)
            s = base + 2 * distance * (2 * up - 1)

            @pl.when((there >= 0) & (there < layers))
            def _(s=s, up=up):
                act(s, up)

    def take_z(s, up):
        along_y(s).wait_recv()
        onward = (z < layers - 1) if up == 0 else (z > 0)

        @pl.when(onward)
        def _():
            along_z(s, 1 - up).start()

        along_y(s).start()

        @pl.when(wanted(s, other))
        def _():
            to_core(s).start()

    def take_y(s, up=0):
        along_y(s).wait_recv()

        @pl.when(wanted(s, other))
        def _():
            to_core(s).start()

    swapped(probe_part, 0).wait_recv()
    use(16 + 8 * c, 7)

    each_side(r, 1, take_z)
    take_y(mate)

    @pl.when(wanted(r, c))
    def _():
        use(2 * r, 2)

    @pl.when(c == 1)
    def _():
        swapped(tail_part, 1).wait_recv()
        use(16, 4)

    each_side(r, 2, take_z)
    each_side(mate, 1, take_y)

    @pl.when(c == 1)
    def _():
        use(20, 4)

    use_chip(mate)
    each_side(r, 1, lambda s, up: use_chip(s))
    each_side(r, 3, take_z)
    each_side(mate, 2, take_y)
    each_side(r, 2, lambda s, up: use_chip(s))
    each_side(mate, 1, lambda s, up: use_chip(s))
    each_side(mate, 3, take_y)
    each_side(r, 3, lambda s, up: use_chip(s))
    each_side(mate, 2, lambda s, up: use_chip(s))
    each_side(mate, 3, lambda s, up: use_chip(s))

    for g in range(4):
        flipped = acc[g].T.astype(st.dtype)
        for half in range(2):
            spot = pl.multiple_of((16 - 8 * c - 2 * g - half) * LANES, LANES)
            st[pl.ds(spot, LANES), :] = flipped[half * LANES:(half + 1) * LANES]
    swap(sketch_part, 2).start()
    mine = (r // 4) == c

    def row_copy():
        return pltpu.make_async_remote_copy(
            acc.at[r % 4], acc.at[4], xsend.at[3], xrecv.at[3],
            device_id={"row": r, "col": other}, device_id_type=MESH)

    @pl.when(mine)
    def _():
        row_copy().start()
        sk_ref[0] = acc[r % 4, :, 0:LANES]
        sk_ref[1] = acc[r % 4, :, LANES:2 * LANES]

    swapped(sketch_part, 2).wait_recv()

    def back_pair(g, carry):
        def add(lag, carry):
            k = 8 * c + jnp.minimum(2 * g + lag, 23)
            spot = pl.multiple_of((16 - lag) * LANES, LANES)
            yacc[...] += jnp.dot(st[pl.ds(spot, 2 * LANES), :], m[k], preferred_element_type=f32)
            return carry

        yacc[...] = jnp.zeros_like(yacc)
        lax.fori_loop(0, 17, add, 0)
        upright = yacc[...].T
        y_ref[2 * g] = upright[:, 0:LANES]
        y_ref[2 * g + 1] = upright[:, LANES:2 * LANES]
        return carry

    lax.fori_loop(0, 5, back_pair, 0)

    @pl.when(jnp.logical_not(mine))
    def _():
        row_copy().wait_recv()
        sk_ref[0] = acc[4, :, 0:LANES]
        sk_ref[1] = acc[4, :, LANES:2 * LANES]

    @pl.when(mine)
    def _():
        row_copy().wait_send()

    def sent(s, up):
        onward = (z < layers - 1) if up == 0 else (z > 0)

        @pl.when(onward)
        def _():
            along_z(s, 1 - up).wait_send()

        along_y(s).wait_send()

        @pl.when(wanted(s, other))
        def _():
            to_core(s).wait_send()

    def sent_core(s, up=0):
        @pl.when(wanted(s, other))
        def _():
            to_core(s).wait_send()

    along_y(r).wait_send()

    @pl.when(z > 0)
    def _():
        along_z(r, 0).wait_send()

    @pl.when(z < layers - 1)
    def _():
        along_z(r, 1).wait_send()

    sent_core(mate)
    for distance in (1, 2, 3):
        each_side(r, distance, sent)
        each_side(mate, distance, sent_core)
    swap(probe_part, 0).wait_send()

    @pl.when(c == 0)
    def _():
        swap(tail_part, 1).wait_send()

    swap(sketch_part, 2).wait_send()


def gathered_body(markov_head, markov_tail, probes):
    order = markov_head.shape[1]
    columns = probes.shape[1]
    blocks = probes.reshape(8, order, columns)[::-1]
    wide = blocks.transpose(1, 0, 2).reshape(order, 8 * columns)
    anywhere = pl.BlockSpec(memory_space=pl.ANY)
    near = pl.BlockSpec(memory_space=pltpu.VMEM)
    dma = pltpu.SemaphoreType.DMA
    sketch, back = pl.pallas_call(
        gathered_kernel,
        out_shape=(jax.ShapeDtypeStruct((2, order, columns), jnp.float32),
                   jax.ShapeDtypeStruct((10, order, columns), jnp.float32)),
        in_specs=[anywhere] * 3,
        out_specs=(near, near),
        scratch_shapes=[
            pltpu.VMEM((32, order, order), jnp.bfloat16),
            pltpu.VMEM((order, 18 * columns), jnp.bfloat16),
            pltpu.VMEM((18 * columns, order), jnp.bfloat16),
            pltpu.VMEM((5, order, 2 * columns), jnp.float32),
            pltpu.VMEM((2 * columns, order), jnp.float32),
            dma((3,)), dma((16,)), dma((8,)), dma((8,)), dma((8,)), dma((8,)), dma((4,)), dma((4,)),
        ],
        compiler_params=pltpu.CompilerParams(
            collective_id=0, has_side_effects=True, vmem_limit_bytes=56 * 1024 * 1024),
    )(markov_head, markov_tail, wide)
    return (sketch.reshape(2 * order, columns),
            back[0:8].reshape(8 * order, columns),
            back[1:9].reshape(8 * order, columns))


def solution(mesh):
    placed = (
        P(("cases", "row"), None, None),
        P(("cases", "col"), None, None),
        P(("cases", "col"), None),
    )
    fits = mesh.shape["row"] == 8 and mesh.shape["col"] == 2

    def parts(markov_head, markov_tail, probes):
        shapes = (markov_head.shape[0], markov_tail.shape[0], probes.shape[1])
        chosen = gathered_body if fits and shapes == (2, 8, LANES) else body
        return chosen(markov_head, markov_tail, probes)

    return jax.shard_map(
        parts,
        mesh=mesh,
        in_specs=placed,
        out_specs=(P(("cases", "row"), None), P(("cases", "col"), None), P(("cases", "col"), None)),
        check_vma=False,
    )
```

```python
import jax
import jax.numpy as jnp
from jax import lax
from jax.experimental import pallas as pl
from jax.experimental.pallas import tpu as pltpu
from jax.sharding import PartitionSpec as P

LANES = 128
MESH = pl.DeviceIdType.MESH
UNROLL = {4: 19, 5: 5}


def spread(x, axis, root):
    mine = lax.axis_index(axis) == root
    return lax.psum(jnp.where(mine, x, jnp.zeros_like(x)), axis)


def from_behind(x, axis, by):
    peers = lax.axis_size(axis)
    pairs = [(i, i + by) for i in range(peers) if 0 <= i + by < peers]
    return lax.ppermute(x, axis, pairs)


def store_slot(window, target, shard):
    slot_count = window.shape[0]
    inside = (target >= 0) & (target < slot_count)
    placed = jnp.clip(target, 0, slot_count - 1)
    present = lax.dynamic_index_in_dim(window, placed, 0, keepdims=False)
    return lax.dynamic_update_index_in_dim(window, jnp.where(inside, shard, present), placed, 0)


def body(markov_head, markov_tail, probes):
    rows_held = markov_head.shape[0]
    order = markov_head.shape[1]
    cols_held = markov_tail.shape[0]
    columns = probes.shape[1]
    row_count = lax.axis_size("row")
    row_place = lax.axis_index("row")
    col_place = lax.axis_index("col")
    strides = cols_held // rows_held
    slot_count = strides + 1
    blocks = probes.reshape(cols_held, order, columns)
    leading = spread(markov_tail, "col", 0)
    full_tail = jnp.concatenate([leading, markov_tail], axis=0)
    window = jnp.zeros((slot_count, rows_held, order, order), markov_head.dtype)

    def march_turn(number, status):
        window_now, carried = status
        window_now = store_slot(window_now, number - col_place * strides, carried)
        carried = from_behind(carried, "row", -1)
        return (window_now, carried)

    window, carried = lax.fori_loop(0, 2 * strides, march_turn, (window, markov_head))
    window = store_slot(window, 2 * strides - col_place * strides, carried)
    shard_ids = row_place + col_place * strides + jnp.arange(slot_count, dtype=jnp.int32)
    offsets = jnp.clip((shard_ids - row_count) * rows_held, 0, 2 * cols_held - rows_held)

    def tail_piece(anchor):
        return lax.dynamic_slice_in_dim(full_tail, anchor, rows_held, 0)

    from_tail = jax.vmap(tail_piece)(offsets)
    window = jnp.where((shard_ids >= row_count)[:, None, None, None], from_tail, window)
    window = window.reshape(slot_count * rows_held, order, order)
    partial_rows = jnp.stack(
        [
            jnp.einsum(
                "jpq,jqk->pk",
                window[offset : offset + cols_held],
                blocks,
                preferred_element_type=jnp.float32,
            )
            for offset in range(rows_held)
        ]
    ).reshape(rows_held * order, columns)
    sketch = lax.psum(partial_rows, "col")
    rounded = sketch.astype(jnp.bfloat16).reshape(rows_held, order, columns)
    current_sum = jnp.zeros((cols_held, order, columns), jnp.float32)
    shifted_sum = jnp.zeros((cols_held, order, columns), jnp.float32)
    for offset in range(rows_held):
        current_sum = current_sum + jnp.einsum(
            "jqp,qk->jpk",
            window[offset : offset + cols_held],
            rounded[offset],
            preferred_element_type=jnp.float32,
        )
        shifted_sum = shifted_sum + jnp.einsum(
            "jqp,qk->jpk",
            window[offset + 1 : offset + 1 + cols_held],
            rounded[offset],
            preferred_element_type=jnp.float32,
        )
    back_now, back_next = lax.psum(
        (
            current_sum.reshape(cols_held * order, columns),
            shifted_sum.reshape(cols_held * order, columns),
        ),
        "row",
    )
    return (sketch, back_now, back_next)


def gathered_kernel(head_ref, tail_ref, probe_ref, sk_ref, now_ref, next_ref, m, px, st, acc, yacc,
                    local_sem, zsend, ysend, ssend, piece_recv, sib_recv, xsend, xrecv):
    f32 = jnp.float32
    r = lax.axis_index("row")
    c = lax.axis_index("col")
    other = 1 - c
    z, y = r // 2, r % 2
    mate = r + 1 - 2 * y
    layers = lax.axis_size("row") // 2

    load_head = pltpu.make_async_copy(head_ref, m.at[pl.ds(2 * r, 2)], local_sem.at[0])
    load_probe = pltpu.make_async_copy(
        probe_ref, px.at[:, pl.ds(pl.multiple_of((12 - 8 * c) * LANES, LANES), 8 * LANES)], local_sem.at[1])
    load_tail = pltpu.make_async_copy(tail_ref, m.at[pl.ds(16 + 8 * c, 8)], local_sem.at[2])
    load_head.start()
    load_probe.start()
    load_tail.start()

    barrier = pltpu.get_barrier_semaphore()

    def greet(row, col):
        pl.semaphore_signal(barrier, inc=1, device_id={"row": row, "col": col}, device_id_type=MESH)

    greet(r, other)
    greet(mate, c)

    @pl.when(z > 0)
    def _():
        greet(r - 2, c)

    @pl.when(z < layers - 1)
    def _():
        greet(r + 2, c)

    zero_columns = jnp.zeros((px.shape[0], 4 * LANES), px.dtype)
    px[:, 0:4 * LANES] = zero_columns
    px[:, 20 * LANES:24 * LANES] = zero_columns
    zero_rows = jnp.zeros((4 * LANES, st.shape[1]), st.dtype)
    st[0:4 * LANES, :] = zero_rows
    st[20 * LANES:24 * LANES, :] = zero_rows
    acc[...] = jnp.zeros_like(acc)
    pl.semaphore_wait(barrier, 2 + (z > 0).astype(jnp.int32) + (z < layers - 1).astype(jnp.int32))

    def along_z(s, up):
        return pltpu.make_async_remote_copy(
            m.at[2 * s + c], m.at[2 * s + c], zsend.at[up * 8 + s], piece_recv.at[s],
            device_id={"row": r + 4 * up - 2, "col": c}, device_id_type=MESH)

    def along_y(s):
        return pltpu.make_async_remote_copy(
            m.at[2 * s + c], m.at[2 * s + c], ysend.at[s], piece_recv.at[s],
            device_id={"row": mate, "col": c}, device_id_type=MESH)

    def to_core(s):
        return pltpu.make_async_remote_copy(
            m.at[2 * s + c], m.at[2 * s + c], ssend.at[s], sib_recv.at[s],
            device_id={"row": r, "col": other}, device_id_type=MESH)

    def from_core(s):
        return pltpu.make_async_remote_copy(
            m.at[2 * s + other], m.at[2 * s + other], ssend.at[s], sib_recv.at[s],
            device_id={"row": r, "col": other}, device_id_type=MESH)

    def swap(ref_of, slot):
        return pltpu.make_async_remote_copy(
            ref_of(c), ref_of(c), xsend.at[slot], xrecv.at[slot],
            device_id={"row": r, "col": other}, device_id_type=MESH)

    def swapped(ref_of, slot):
        return pltpu.make_async_remote_copy(
            ref_of(other), ref_of(other), xsend.at[slot], xrecv.at[slot],
            device_id={"row": r, "col": other}, device_id_type=MESH)

    def probe_part(core):
        return px.at[:, pl.ds(pl.multiple_of((12 - 8 * core) * LANES, LANES), 8 * LANES)]

    def tail_part(core):
        return m.at[pl.ds(16 + 8 * core, 8)]

    def sketch_part(core):
        return st.at[pl.ds(pl.multiple_of((12 - 8 * core) * LANES, LANES), 8 * LANES), :]

    load_head.wait()
    along_y(r).start()

    @pl.when(z > 0)
    def _():
        along_z(r, 0).start()

    @pl.when(z < layers - 1)
    def _():
        along_z(r, 1).start()

    load_probe.wait()
    swap(probe_part, 0).start()
    load_tail.wait()

    @pl.when(c == 0)
    def _():
        swap(tail_part, 1).start()

    def use(first, count):
        def turn(step, carry):
            k = first + step // 4
            g = step % 4
            lag = k - 8 * c - 2 * g

            @pl.when((lag >= 0) & (lag <= 16))
            def _():
                spot = pl.multiple_of((19 - lag) * LANES, LANES)
                acc[g] += jnp.dot(m[k], px[:, pl.ds(spot, 2 * LANES)], preferred_element_type=f32)

            return carry

        lax.fori_loop(0, 4 * count, turn, 0)

    def wanted(s, core):
        return (core == 0) | (s >= 4)

    def use_chip(s):
        @pl.when(wanted(s, c))
        def _():
            from_core(s).wait_recv()
            use(2 * s, 2)

    def each_side(base, distance, act):
        for up in (0, 1):
            there = z + distance * (2 * up - 1)
            s = base + 2 * distance * (2 * up - 1)

            @pl.when((there >= 0) & (there < layers))
            def _(s=s, up=up):
                act(s, up)

    def take_z(s, up):
        along_y(s).wait_recv()
        onward = (z < layers - 1) if up == 0 else (z > 0)

        @pl.when(onward)
        def _():
            along_z(s, 1 - up).start()

        along_y(s).start()

        @pl.when(wanted(s, other))
        def _():
            to_core(s).start()

    def take_y(s, up=0):
        along_y(s).wait_recv()

        @pl.when(wanted(s, other))
        def _():
            to_core(s).start()

    swapped(probe_part, 0).wait_recv()
    use(16 + 8 * c, 7)

    each_side(r, 1, take_z)
    take_y(mate)

    @pl.when(wanted(r, c))
    def _():
        use(2 * r, 2)

    @pl.when(c == 1)
    def _():
        swapped(tail_part, 1).wait_recv()
        use(16, 4)

    each_side(r, 2, take_z)
    each_side(mate, 1, take_y)

    @pl.when(c == 1)
    def _():
        use(20, 4)

    use_chip(mate)
    each_side(r, 1, lambda s, up: use_chip(s))
    each_side(r, 3, take_z)
    each_side(mate, 2, take_y)
    each_side(r, 2, lambda s, up: use_chip(s))
    each_side(mate, 1, lambda s, up: use_chip(s))
    each_side(mate, 3, take_y)
    each_side(r, 3, lambda s, up: use_chip(s))
    each_side(mate, 2, lambda s, up: use_chip(s))
    each_side(mate, 3, lambda s, up: use_chip(s))

    for g in range(4):
        flipped = acc[g].T.astype(st.dtype)
        for half in range(2):
            spot = pl.multiple_of((19 - 8 * c - 2 * g - half) * LANES, LANES)
            st[pl.ds(spot, LANES), :] = flipped[half * LANES:(half + 1) * LANES]
    swap(sketch_part, 2).start()
    mine = (r // 4) == c
    order = acc.shape[1]

    def row_copy():
        return pltpu.make_async_remote_copy(
            acc.at[r % 4], acc.at[4], xsend.at[3], xrecv.at[3],
            device_id={"row": r, "col": other}, device_id_type=MESH)

    @pl.when(mine)
    def _():
        row_copy().start()
        sk_ref[0:order] = acc[r % 4, :, 0:LANES]
        sk_ref[order:2 * order] = acc[r % 4, :, LANES:2 * LANES]

    swapped(sketch_part, 2).wait_recv()

    for first, wide in ((0, 4), (4, 5)):
        rows = wide * LANES

        def add(turn, carry, first=first, wide=wide, rows=rows):
            total = None
            for part in range(UNROLL[wide]):
                lag = UNROLL[wide] * turn + part
                spot = pl.multiple_of((19 - lag) * LANES, LANES)
                term = jnp.dot(st[pl.ds(spot, rows), :], m[8 * c + first + lag], preferred_element_type=f32)
                total = term if total is None else total + term
            yacc[0:rows] += total
            return carry

        yacc[0:rows] = jnp.zeros((rows, yacc.shape[1]), f32)
        lax.fori_loop(0, (15 + wide) // UNROLL[wide], add, 0)
        for block in range(first, first + wide):
            upright = yacc[(block - first) * LANES:(block - first + 1) * LANES].T
            if block < 8:
                now_ref[block * order:(block + 1) * order] = upright
            if block > 0:
                next_ref[(block - 1) * order:block * order] = upright

    @pl.when(jnp.logical_not(mine))
    def _():
        row_copy().wait_recv()
        sk_ref[0:order] = acc[4, :, 0:LANES]
        sk_ref[order:2 * order] = acc[4, :, LANES:2 * LANES]

    @pl.when(mine)
    def _():
        row_copy().wait_send()

    def sent(s, up):
        onward = (z < layers - 1) if up == 0 else (z > 0)

        @pl.when(onward)
        def _():
            along_z(s, 1 - up).wait_send()

        along_y(s).wait_send()

        @pl.when(wanted(s, other))
        def _():
            to_core(s).wait_send()

    def sent_core(s, up=0):
        @pl.when(wanted(s, other))
        def _():
            to_core(s).wait_send()

    along_y(r).wait_send()

    @pl.when(z > 0)
    def _():
        along_z(r, 0).wait_send()

    @pl.when(z < layers - 1)
    def _():
        along_z(r, 1).wait_send()

    sent_core(mate)
    for distance in (1, 2, 3):
        each_side(r, distance, sent)
        each_side(mate, distance, sent_core)
    swap(probe_part, 0).wait_send()

    @pl.when(c == 0)
    def _():
        swap(tail_part, 1).wait_send()

    swap(sketch_part, 2).wait_send()


def gathered_body(markov_head, markov_tail, probes):
    order = markov_head.shape[1]
    columns = probes.shape[1]
    blocks = probes.reshape(8, order, columns)[::-1]
    wide = blocks.transpose(1, 0, 2).reshape(order, 8 * columns)
    anywhere = pl.BlockSpec(memory_space=pl.ANY)
    near = pl.BlockSpec(memory_space=pltpu.VMEM)
    dma = pltpu.SemaphoreType.DMA
    return pl.pallas_call(
        gathered_kernel,
        out_shape=(jax.ShapeDtypeStruct((2 * order, columns), jnp.float32),
                   jax.ShapeDtypeStruct((8 * order, columns), jnp.float32),
                   jax.ShapeDtypeStruct((8 * order, columns), jnp.float32)),
        in_specs=[anywhere] * 3,
        out_specs=(near, near, near),
        scratch_shapes=[
            pltpu.VMEM((32, order, order), jnp.bfloat16),
            pltpu.VMEM((order, 24 * columns), jnp.bfloat16),
            pltpu.VMEM((24 * columns, order), jnp.bfloat16),
            pltpu.VMEM((5, order, 2 * columns), jnp.float32),
            pltpu.VMEM((5 * columns, order), jnp.float32),
            dma((3,)), dma((16,)), dma((8,)), dma((8,)), dma((8,)), dma((8,)), dma((4,)), dma((4,)),
        ],
        compiler_params=pltpu.CompilerParams(
            collective_id=0, has_side_effects=True, vmem_limit_bytes=56 * 1024 * 1024),
    )(markov_head, markov_tail, wide)


def solution(mesh):
    placed = (
        P(("cases", "row"), None, None),
        P(("cases", "col"), None, None),
        P(("cases", "col"), None),
    )
    fits = mesh.shape["row"] == 8 and mesh.shape["col"] == 2

    def parts(markov_head, markov_tail, probes):
        shapes = (markov_head.shape[0], markov_tail.shape[0], probes.shape[1])
        chosen = gathered_body if fits and shapes == (2, 8, LANES) else body
        return chosen(markov_head, markov_tail, probes)

    return jax.shard_map(
        parts,
        mesh=mesh,
        in_specs=placed,
        out_specs=(P(("cases", "row"), None), P(("cases", "col"), None), P(("cases", "col"), None)),
        check_vma=False,
    )
```

```python
import jax
import jax.numpy as jnp
from jax import lax
from jax.experimental import pallas as pl
from jax.experimental.pallas import tpu as pltpu
from jax.sharding import PartitionSpec as P

LANES = 128
MESH = pl.DeviceIdType.MESH
UNROLL = {4: 19, 5: 5}


def spread(x, axis, root):
    mine = lax.axis_index(axis) == root
    return lax.psum(jnp.where(mine, x, jnp.zeros_like(x)), axis)


def from_behind(x, axis, by):
    peers = lax.axis_size(axis)
    pairs = [(i, i + by) for i in range(peers) if 0 <= i + by < peers]
    return lax.ppermute(x, axis, pairs)


def store_slot(window, target, shard):
    slot_count = window.shape[0]
    inside = (target >= 0) & (target < slot_count)
    placed = jnp.clip(target, 0, slot_count - 1)
    present = lax.dynamic_index_in_dim(window, placed, 0, keepdims=False)
    return lax.dynamic_update_index_in_dim(window, jnp.where(inside, shard, present), placed, 0)


def body(markov_head, markov_tail, probes):
    rows_held = markov_head.shape[0]
    order = markov_head.shape[1]
    cols_held = markov_tail.shape[0]
    columns = probes.shape[1]
    row_count = lax.axis_size("row")
    row_place = lax.axis_index("row")
    col_place = lax.axis_index("col")
    strides = cols_held // rows_held
    slot_count = strides + 1
    blocks = probes.reshape(cols_held, order, columns)
    leading = spread(markov_tail, "col", 0)
    full_tail = jnp.concatenate([leading, markov_tail], axis=0)
    window = jnp.zeros((slot_count, rows_held, order, order), markov_head.dtype)

    def march_turn(number, status):
        window_now, carried = status
        window_now = store_slot(window_now, number - col_place * strides, carried)
        carried = from_behind(carried, "row", -1)
        return (window_now, carried)

    window, carried = lax.fori_loop(0, 2 * strides, march_turn, (window, markov_head))
    window = store_slot(window, 2 * strides - col_place * strides, carried)
    shard_ids = row_place + col_place * strides + jnp.arange(slot_count, dtype=jnp.int32)
    offsets = jnp.clip((shard_ids - row_count) * rows_held, 0, 2 * cols_held - rows_held)

    def tail_piece(anchor):
        return lax.dynamic_slice_in_dim(full_tail, anchor, rows_held, 0)

    from_tail = jax.vmap(tail_piece)(offsets)
    window = jnp.where((shard_ids >= row_count)[:, None, None, None], from_tail, window)
    window = window.reshape(slot_count * rows_held, order, order)
    partial_rows = jnp.stack(
        [
            jnp.einsum(
                "jpq,jqk->pk",
                window[offset : offset + cols_held],
                blocks,
                preferred_element_type=jnp.float32,
            )
            for offset in range(rows_held)
        ]
    ).reshape(rows_held * order, columns)
    sketch = lax.psum(partial_rows, "col")
    rounded = sketch.astype(jnp.bfloat16).reshape(rows_held, order, columns)
    current_sum = jnp.zeros((cols_held, order, columns), jnp.float32)
    shifted_sum = jnp.zeros((cols_held, order, columns), jnp.float32)
    for offset in range(rows_held):
        current_sum = current_sum + jnp.einsum(
            "jqp,qk->jpk",
            window[offset : offset + cols_held],
            rounded[offset],
            preferred_element_type=jnp.float32,
        )
        shifted_sum = shifted_sum + jnp.einsum(
            "jqp,qk->jpk",
            window[offset + 1 : offset + 1 + cols_held],
            rounded[offset],
            preferred_element_type=jnp.float32,
        )
    back_now, back_next = lax.psum(
        (
            current_sum.reshape(cols_held * order, columns),
            shifted_sum.reshape(cols_held * order, columns),
        ),
        "row",
    )
    return (sketch, back_now, back_next)


def gathered_kernel(head_ref, tail_ref, probe_ref, sk_ref, now_ref, next_ref, m, px, st, acc, yacc, head_in, tail_in, probe_in,
                    local_sem, zsend, ysend, ssend, piece_recv, sib_recv, xsend, xrecv):
    f32 = jnp.float32
    order = acc.shape[1]
    r = lax.axis_index("row")
    c = lax.axis_index("col")
    other = 1 - c
    z, y = r // 2, r % 2
    mate = r + 1 - 2 * y
    layers = lax.axis_size("row") // 2

    load_head = pltpu.make_async_copy(head_ref, head_in, local_sem.at[0])
    load_probe = pltpu.make_async_copy(probe_ref, probe_in, local_sem.at[1])
    load_tail = pltpu.make_async_copy(tail_ref, tail_in, local_sem.at[2])
    load_head.start()
    load_probe.start()
    load_tail.start()

    barrier = pltpu.get_barrier_semaphore()

    def greet(row, col):
        pl.semaphore_signal(barrier, inc=1, device_id={"row": row, "col": col}, device_id_type=MESH)

    greet(r, other)
    greet(mate, c)

    @pl.when(z > 0)
    def _():
        greet(r - 2, c)

    @pl.when(z < layers - 1)
    def _():
        greet(r + 2, c)

    zero_columns = jnp.zeros((px.shape[0], 4 * LANES), px.dtype)
    px[:, 0:4 * LANES] = zero_columns
    px[:, 20 * LANES:24 * LANES] = zero_columns
    zero_rows = jnp.zeros((4 * LANES, st.shape[1]), st.dtype)
    st[0:4 * LANES, :] = zero_rows
    st[20 * LANES:24 * LANES, :] = zero_rows
    acc[...] = jnp.zeros_like(acc)
    pl.semaphore_wait(barrier, 2 + (z > 0).astype(jnp.int32) + (z < layers - 1).astype(jnp.int32))

    def along_z(s, up):
        return pltpu.make_async_remote_copy(
            m.at[2 * s + c], m.at[2 * s + c], zsend.at[up * 8 + s], piece_recv.at[s],
            device_id={"row": r + 4 * up - 2, "col": c}, device_id_type=MESH)

    def along_y(s):
        return pltpu.make_async_remote_copy(
            m.at[2 * s + c], m.at[2 * s + c], ysend.at[s], piece_recv.at[s],
            device_id={"row": mate, "col": c}, device_id_type=MESH)

    def to_core(s):
        return pltpu.make_async_remote_copy(
            m.at[2 * s + c], m.at[2 * s + c], ssend.at[s], sib_recv.at[s],
            device_id={"row": r, "col": other}, device_id_type=MESH)

    def from_core(s):
        return pltpu.make_async_remote_copy(
            m.at[2 * s + other], m.at[2 * s + other], ssend.at[s], sib_recv.at[s],
            device_id={"row": r, "col": other}, device_id_type=MESH)

    def swap(ref_of, slot):
        return pltpu.make_async_remote_copy(
            ref_of(c), ref_of(c), xsend.at[slot], xrecv.at[slot],
            device_id={"row": r, "col": other}, device_id_type=MESH)

    def swapped(ref_of, slot):
        return pltpu.make_async_remote_copy(
            ref_of(other), ref_of(other), xsend.at[slot], xrecv.at[slot],
            device_id={"row": r, "col": other}, device_id_type=MESH)

    def probe_part(core):
        return px.at[:, pl.ds(pl.multiple_of((12 - 8 * core) * LANES, LANES), 8 * LANES)]

    def tail_part(core):
        return m.at[pl.ds(16 + 8 * core, 8)]

    def sketch_part(core):
        return st.at[pl.ds(pl.multiple_of((12 - 8 * core) * LANES, LANES), 8 * LANES), :]

    load_head.wait()
    for half in range(2):
        m[2 * r + half] = head_in[:, half, :]
    along_y(r).start()

    @pl.when(z > 0)
    def _():
        along_z(r, 0).start()

    @pl.when(z < layers - 1)
    def _():
        along_z(r, 1).start()

    load_probe.wait()
    for j in range(8):
        spot = pl.multiple_of((19 - 8 * c - j) * LANES, LANES)
        px[:, pl.ds(spot, LANES)] = probe_in[j * order:(j + 1) * order, :]
    swap(probe_part, 0).start()
    load_tail.wait()
    for j in range(8):
        m[16 + 8 * c + j] = tail_in[:, j, :]

    @pl.when(c == 0)
    def _():
        swap(tail_part, 1).start()

    def use(first, count):
        def turn(step, carry):
            k = first + step // 4
            g = step % 4
            lag = k - 8 * c - 2 * g

            @pl.when((lag >= 0) & (lag <= 16))
            def _():
                spot = pl.multiple_of((19 - lag) * LANES, LANES)
                acc[g] += jnp.dot(m[k], px[:, pl.ds(spot, 2 * LANES)], preferred_element_type=f32)

            return carry

        lax.fori_loop(0, 4 * count, turn, 0)

    def wanted(s, core):
        return (core == 0) | (s >= 4)

    def use_chip(s):
        @pl.when(wanted(s, c))
        def _():
            from_core(s).wait_recv()
            use(2 * s, 2)

    def each_side(base, distance, act):
        for up in (0, 1):
            there = z + distance * (2 * up - 1)
            s = base + 2 * distance * (2 * up - 1)

            @pl.when((there >= 0) & (there < layers))
            def _(s=s, up=up):
                act(s, up)

    def take_z(s, up):
        along_y(s).wait_recv()
        onward = (z < layers - 1) if up == 0 else (z > 0)

        @pl.when(onward)
        def _():
            along_z(s, 1 - up).start()

        along_y(s).start()

        @pl.when(wanted(s, other))
        def _():
            to_core(s).start()

    def take_y(s, up=0):
        along_y(s).wait_recv()

        @pl.when(wanted(s, other))
        def _():
            to_core(s).start()

    swapped(probe_part, 0).wait_recv()
    use(16 + 8 * c, 7)

    each_side(r, 1, take_z)
    take_y(mate)

    @pl.when(wanted(r, c))
    def _():
        use(2 * r, 2)

    @pl.when(c == 1)
    def _():
        swapped(tail_part, 1).wait_recv()
        use(16, 4)

    each_side(r, 2, take_z)
    each_side(mate, 1, take_y)

    @pl.when(c == 1)
    def _():
        use(20, 4)

    use_chip(mate)
    each_side(r, 1, lambda s, up: use_chip(s))
    each_side(r, 3, take_z)
    each_side(mate, 2, take_y)
    each_side(r, 2, lambda s, up: use_chip(s))
    each_side(mate, 1, lambda s, up: use_chip(s))
    each_side(mate, 3, take_y)
    each_side(r, 3, lambda s, up: use_chip(s))
    each_side(mate, 2, lambda s, up: use_chip(s))
    each_side(mate, 3, lambda s, up: use_chip(s))

    for g in range(4):
        flipped = acc[g].T.astype(st.dtype)
        for half in range(2):
            spot = pl.multiple_of((19 - 8 * c - 2 * g - half) * LANES, LANES)
            st[pl.ds(spot, LANES), :] = flipped[half * LANES:(half + 1) * LANES]
    swap(sketch_part, 2).start()
    mine = (r // 4) == c

    def row_copy():
        return pltpu.make_async_remote_copy(
            acc.at[r % 4], acc.at[4], xsend.at[3], xrecv.at[3],
            device_id={"row": r, "col": other}, device_id_type=MESH)

    @pl.when(mine)
    def _():
        row_copy().start()
        sk_ref[0:order] = acc[r % 4, :, 0:LANES]
        sk_ref[order:2 * order] = acc[r % 4, :, LANES:2 * LANES]

    swapped(sketch_part, 2).wait_recv()

    for first, wide in ((0, 4), (4, 5)):
        rows = wide * LANES

        def add(turn, carry, first=first, wide=wide, rows=rows):
            total = None
            for part in range(UNROLL[wide]):
                lag = UNROLL[wide] * turn + part
                spot = pl.multiple_of((19 - lag) * LANES, LANES)
                term = jnp.dot(st[pl.ds(spot, rows), :], m[8 * c + first + lag], preferred_element_type=f32)
                total = term if total is None else total + term
            yacc[0:rows] += total
            return carry

        yacc[0:rows] = jnp.zeros((rows, yacc.shape[1]), f32)
        lax.fori_loop(0, (15 + wide) // UNROLL[wide], add, 0)
        for block in range(first, first + wide):
            upright = yacc[(block - first) * LANES:(block - first + 1) * LANES].T
            if block < 8:
                now_ref[block * order:(block + 1) * order] = upright
            if block > 0:
                next_ref[(block - 1) * order:block * order] = upright

    @pl.when(jnp.logical_not(mine))
    def _():
        row_copy().wait_recv()
        sk_ref[0:order] = acc[4, :, 0:LANES]
        sk_ref[order:2 * order] = acc[4, :, LANES:2 * LANES]

    @pl.when(mine)
    def _():
        row_copy().wait_send()

    def sent(s, up):
        onward = (z < layers - 1) if up == 0 else (z > 0)

        @pl.when(onward)
        def _():
            along_z(s, 1 - up).wait_send()

        along_y(s).wait_send()

        @pl.when(wanted(s, other))
        def _():
            to_core(s).wait_send()

    def sent_core(s, up=0):
        @pl.when(wanted(s, other))
        def _():
            to_core(s).wait_send()

    along_y(r).wait_send()

    @pl.when(z > 0)
    def _():
        along_z(r, 0).wait_send()

    @pl.when(z < layers - 1)
    def _():
        along_z(r, 1).wait_send()

    sent_core(mate)
    for distance in (1, 2, 3):
        each_side(r, distance, sent)
        each_side(mate, distance, sent_core)
    swap(probe_part, 0).wait_send()

    @pl.when(c == 0)
    def _():
        swap(tail_part, 1).wait_send()

    swap(sketch_part, 2).wait_send()


def gathered_body(markov_head, markov_tail, probes):
    order = markov_head.shape[1]
    columns = probes.shape[1]
    anywhere = pl.BlockSpec(memory_space=pl.ANY)
    near = pl.BlockSpec(memory_space=pltpu.VMEM)
    dma = pltpu.SemaphoreType.DMA
    return pl.pallas_call(
        gathered_kernel,
        out_shape=(jax.ShapeDtypeStruct((2 * order, columns), jnp.float32),
                   jax.ShapeDtypeStruct((8 * order, columns), jnp.float32),
                   jax.ShapeDtypeStruct((8 * order, columns), jnp.float32)),
        in_specs=[anywhere] * 3,
        out_specs=(near, near, near),
        scratch_shapes=[
            pltpu.VMEM((32, order, order), jnp.bfloat16),
            pltpu.VMEM((order, 24 * columns), jnp.bfloat16),
            pltpu.VMEM((24 * columns, order), jnp.bfloat16),
            pltpu.VMEM((5, order, 2 * columns), jnp.float32),
            pltpu.VMEM((5 * columns, order), jnp.float32),
            pltpu.VMEM((order, 2, order), jnp.bfloat16),
            pltpu.VMEM((order, 8, order), jnp.bfloat16),
            pltpu.VMEM((8 * order, columns), jnp.bfloat16),
            dma((3,)), dma((16,)), dma((8,)), dma((8,)), dma((8,)), dma((8,)), dma((4,)), dma((4,)),
        ],
        compiler_params=pltpu.CompilerParams(
            collective_id=0, has_side_effects=True, vmem_limit_bytes=56 * 1024 * 1024),
    )(markov_head.transpose(1, 0, 2), markov_tail.transpose(1, 0, 2), probes)


def solution(mesh):
    placed = (
        P(("cases", "row"), None, None),
        P(("cases", "col"), None, None),
        P(("cases", "col"), None),
    )
    fits = mesh.shape["row"] == 8 and mesh.shape["col"] == 2

    def parts(markov_head, markov_tail, probes):
        shapes = (markov_head.shape[0], markov_tail.shape[0], probes.shape[1])
        chosen = gathered_body if fits and shapes == (2, 8, LANES) else body
        return chosen(markov_head, markov_tail, probes)

    return jax.shard_map(
        parts,
        mesh=mesh,
        in_specs=placed,
        out_specs=(P(("cases", "row"), None), P(("cases", "col"), None), P(("cases", "col"), None)),
        check_vma=False,
    )
```

```python
import jax
import jax.numpy as jnp
from jax import lax
from jax.experimental import pallas as pl
from jax.experimental.pallas import tpu as pltpu
from jax.sharding import PartitionSpec as P

LANES = 128
MESH = pl.DeviceIdType.MESH
UNROLL = {4: 19, 5: 5}


def spread(x, axis, root):
    mine = lax.axis_index(axis) == root
    return lax.psum(jnp.where(mine, x, jnp.zeros_like(x)), axis)


def from_behind(x, axis, by):
    peers = lax.axis_size(axis)
    pairs = [(i, i + by) for i in range(peers) if 0 <= i + by < peers]
    return lax.ppermute(x, axis, pairs)


def store_slot(window, target, shard):
    slot_count = window.shape[0]
    inside = (target >= 0) & (target < slot_count)
    placed = jnp.clip(target, 0, slot_count - 1)
    present = lax.dynamic_index_in_dim(window, placed, 0, keepdims=False)
    return lax.dynamic_update_index_in_dim(window, jnp.where(inside, shard, present), placed, 0)


def body(markov_head, markov_tail, probes):
    rows_held = markov_head.shape[0]
    order = markov_head.shape[1]
    cols_held = markov_tail.shape[0]
    columns = probes.shape[1]
    row_count = lax.axis_size("row")
    row_place = lax.axis_index("row")
    col_place = lax.axis_index("col")
    strides = cols_held // rows_held
    slot_count = strides + 1
    blocks = probes.reshape(cols_held, order, columns)
    leading = spread(markov_tail, "col", 0)
    full_tail = jnp.concatenate([leading, markov_tail], axis=0)
    window = jnp.zeros((slot_count, rows_held, order, order), markov_head.dtype)

    def march_turn(number, status):
        window_now, carried = status
        window_now = store_slot(window_now, number - col_place * strides, carried)
        carried = from_behind(carried, "row", -1)
        return (window_now, carried)

    window, carried = lax.fori_loop(0, 2 * strides, march_turn, (window, markov_head))
    window = store_slot(window, 2 * strides - col_place * strides, carried)
    shard_ids = row_place + col_place * strides + jnp.arange(slot_count, dtype=jnp.int32)
    offsets = jnp.clip((shard_ids - row_count) * rows_held, 0, 2 * cols_held - rows_held)

    def tail_piece(anchor):
        return lax.dynamic_slice_in_dim(full_tail, anchor, rows_held, 0)

    from_tail = jax.vmap(tail_piece)(offsets)
    window = jnp.where((shard_ids >= row_count)[:, None, None, None], from_tail, window)
    window = window.reshape(slot_count * rows_held, order, order)
    partial_rows = jnp.stack(
        [
            jnp.einsum(
                "jpq,jqk->pk",
                window[offset : offset + cols_held],
                blocks,
                preferred_element_type=jnp.float32,
            )
            for offset in range(rows_held)
        ]
    ).reshape(rows_held * order, columns)
    sketch = lax.psum(partial_rows, "col")
    rounded = sketch.astype(jnp.bfloat16).reshape(rows_held, order, columns)
    current_sum = jnp.zeros((cols_held, order, columns), jnp.float32)
    shifted_sum = jnp.zeros((cols_held, order, columns), jnp.float32)
    for offset in range(rows_held):
        current_sum = current_sum + jnp.einsum(
            "jqp,qk->jpk",
            window[offset : offset + cols_held],
            rounded[offset],
            preferred_element_type=jnp.float32,
        )
        shifted_sum = shifted_sum + jnp.einsum(
            "jqp,qk->jpk",
            window[offset + 1 : offset + 1 + cols_held],
            rounded[offset],
            preferred_element_type=jnp.float32,
        )
    back_now, back_next = lax.psum(
        (
            current_sum.reshape(cols_held * order, columns),
            shifted_sum.reshape(cols_held * order, columns),
        ),
        "row",
    )
    return (sketch, back_now, back_next)


def gathered_kernel(head_ref, tail_ref, probe_ref, sk_ref, now_ref, next_ref, m, px, st, acc, yacc, head_in, tail_in, probe_in,
                    local_sem, zsend, ysend, ssend, piece_recv, sib_recv, xsend, xrecv):
    f32 = jnp.float32
    order = acc.shape[1]
    r = lax.axis_index("row")
    c = lax.axis_index("col")
    other = 1 - c
    z, y = r // 2, r % 2
    mate = r + 1 - 2 * y
    layers = lax.axis_size("row") // 2

    load_head = pltpu.make_async_copy(head_ref, head_in, local_sem.at[0])
    load_probe = pltpu.make_async_copy(probe_ref, probe_in, local_sem.at[1])
    load_tail = pltpu.make_async_copy(tail_ref, tail_in, local_sem.at[2])
    load_head.start()
    load_probe.start()
    load_tail.start()

    barrier = pltpu.get_barrier_semaphore()

    def greet(row, col):
        pl.semaphore_signal(barrier, inc=1, device_id={"row": row, "col": col}, device_id_type=MESH)

    greet(r, other)
    greet(mate, c)

    @pl.when(z > 0)
    def _():
        greet(r - 2, c)

    @pl.when(z < layers - 1)
    def _():
        greet(r + 2, c)

    zero_columns = jnp.zeros((px.shape[0], 4 * LANES), px.dtype)
    px[:, 0:4 * LANES] = zero_columns
    px[:, 20 * LANES:24 * LANES] = zero_columns
    zero_rows = jnp.zeros((4 * LANES, st.shape[1]), st.dtype)
    st[0:4 * LANES, :] = zero_rows
    st[20 * LANES:24 * LANES, :] = zero_rows
    acc[...] = jnp.zeros_like(acc)
    pl.semaphore_wait(barrier, 2 + (z > 0).astype(jnp.int32) + (z < layers - 1).astype(jnp.int32))

    def piece(k, h):
        return m.at[k, pl.ds(256 * h, 256)]

    def along_z(s, up, h):
        return pltpu.make_async_remote_copy(
            piece(2 * s + c, h), piece(2 * s + c, h), zsend.at[16 * up + 2 * s + h], piece_recv.at[2 * s + h],
            device_id={"row": r + 4 * up - 2, "col": c}, device_id_type=MESH)

    def along_y(s, h):
        return pltpu.make_async_remote_copy(
            piece(2 * s + c, h), piece(2 * s + c, h), ysend.at[2 * s + h], piece_recv.at[2 * s + h],
            device_id={"row": mate, "col": c}, device_id_type=MESH)

    def to_core(s, h):
        return pltpu.make_async_remote_copy(
            piece(2 * s + c, h), piece(2 * s + c, h), ssend.at[2 * s + h], sib_recv.at[2 * s + h],
            device_id={"row": r, "col": other}, device_id_type=MESH)

    def from_core(s, h):
        return pltpu.make_async_remote_copy(
            piece(2 * s + other, h), piece(2 * s + other, h), ssend.at[2 * s + h], sib_recv.at[2 * s + h],
            device_id={"row": r, "col": other}, device_id_type=MESH)

    def swap(ref_of, slot):
        return pltpu.make_async_remote_copy(
            ref_of(c), ref_of(c), xsend.at[slot], xrecv.at[slot],
            device_id={"row": r, "col": other}, device_id_type=MESH)

    def swapped(ref_of, slot):
        return pltpu.make_async_remote_copy(
            ref_of(other), ref_of(other), xsend.at[slot], xrecv.at[slot],
            device_id={"row": r, "col": other}, device_id_type=MESH)

    def probe_part(core):
        return px.at[:, pl.ds(pl.multiple_of((12 - 8 * core) * LANES, LANES), 8 * LANES)]

    def tail_part(core):
        return m.at[pl.ds(16 + 8 * core, 8)]

    def sketch_part(core):
        return st.at[pl.ds(pl.multiple_of((12 - 8 * core) * LANES, LANES), 8 * LANES), :]

    load_head.wait()
    for half in range(2):
        m[2 * r + half, 0:order] = head_in[:, half, :]
    for h in (0, 1):
        along_y(r, h).start()

        @pl.when(z > 0)
        def _(h=h):
            along_z(r, 0, h).start()

        @pl.when(z < layers - 1)
        def _(h=h):
            along_z(r, 1, h).start()

    load_probe.wait()
    for j in range(8):
        spot = pl.multiple_of((19 - 8 * c - j) * LANES, LANES)
        px[:, pl.ds(spot, LANES)] = probe_in[j * order:(j + 1) * order, :]
    swap(probe_part, 0).start()
    load_tail.wait()
    for j in range(8):
        m[16 + 8 * c + j, 0:order] = tail_in[:, j, :]

    @pl.when(c == 0)
    def _():
        swap(tail_part, 1).start()

    def use(first, count):
        def turn(step, carry):
            k = first + step // 4
            g = step % 4
            lag = k - 8 * c - 2 * g

            @pl.when((lag >= 0) & (lag <= 16))
            def _():
                spot = pl.multiple_of((19 - lag) * LANES, LANES)
                acc[g] += jnp.dot(m[k, 0:order], px[:, pl.ds(spot, 2 * LANES)], preferred_element_type=f32)

            return carry

        lax.fori_loop(0, 4 * count, turn, 0)

    def wanted(s, core):
        return (core == 0) | (s >= 4)

    def use_chip(s):
        @pl.when(wanted(s, c))
        def _():
            from_core(s, 0).wait_recv()
            from_core(s, 1).wait_recv()
            use(2 * s, 2)

    def each_side(base, distance, act):
        for up in (0, 1):
            there = z + distance * (2 * up - 1)
            s = base + 2 * distance * (2 * up - 1)

            @pl.when((there >= 0) & (there < layers))
            def _(s=s, up=up):
                act(s, up)

    def take_z(s, up, h):
        along_y(s, h).wait_recv()
        onward = (z < layers - 1) if up == 0 else (z > 0)

        @pl.when(onward)
        def _():
            along_z(s, 1 - up, h).start()

        along_y(s, h).start()

        @pl.when(wanted(s, other))
        def _():
            to_core(s, h).start()

    def take_y(s, h):
        along_y(s, h).wait_recv()

        @pl.when(wanted(s, other))
        def _():
            to_core(s, h).start()

    def arrive(distance, h):
        each_side(r, distance, lambda s, up: take_z(s, up, h))
        if distance == 1:
            take_y(mate, h)
        else:
            each_side(mate, distance - 1, lambda s, up: take_y(s, h))

    swapped(probe_part, 0).wait_recv()
    use(16 + 8 * c, 7)

    arrive(1, 0)

    @pl.when(wanted(r, c))
    def _():
        use(2 * r, 2)

    arrive(1, 1)

    @pl.when(c == 1)
    def _():
        swapped(tail_part, 1).wait_recv()
        use(16, 4)

    arrive(2, 0)

    @pl.when(c == 1)
    def _():
        use(20, 4)

    arrive(2, 1)
    use_chip(mate)
    each_side(r, 1, lambda s, up: use_chip(s))
    arrive(3, 0)
    each_side(r, 2, lambda s, up: use_chip(s))
    arrive(3, 1)
    each_side(mate, 1, lambda s, up: use_chip(s))
    each_side(mate, 3, lambda s, up: take_y(s, 0))
    each_side(r, 3, lambda s, up: use_chip(s))
    each_side(mate, 2, lambda s, up: use_chip(s))
    each_side(mate, 3, lambda s, up: take_y(s, 1))
    each_side(mate, 3, lambda s, up: use_chip(s))

    for g in range(4):
        flipped = acc[g].T.astype(st.dtype)
        for half in range(2):
            spot = pl.multiple_of((19 - 8 * c - 2 * g - half) * LANES, LANES)
            st[pl.ds(spot, LANES), :] = flipped[half * LANES:(half + 1) * LANES]
    swap(sketch_part, 2).start()
    mine = (r // 4) == c

    def row_copy():
        return pltpu.make_async_remote_copy(
            acc.at[r % 4], acc.at[4], xsend.at[3], xrecv.at[3],
            device_id={"row": r, "col": other}, device_id_type=MESH)

    @pl.when(mine)
    def _():
        row_copy().start()
        sk_ref[0:order] = acc[r % 4, :, 0:LANES]
        sk_ref[order:2 * order] = acc[r % 4, :, LANES:2 * LANES]

    swapped(sketch_part, 2).wait_recv()

    for first, wide in ((0, 4), (4, 5)):
        rows = wide * LANES

        def add(turn, carry, first=first, wide=wide, rows=rows):
            total = None
            for part in range(UNROLL[wide]):
                lag = UNROLL[wide] * turn + part
                spot = pl.multiple_of((19 - lag) * LANES, LANES)
                term = jnp.dot(st[pl.ds(spot, rows), :], m[8 * c + first + lag, 0:order], preferred_element_type=f32)
                total = term if total is None else total + term
            yacc[0:rows] += total
            return carry

        yacc[0:rows] = jnp.zeros((rows, yacc.shape[1]), f32)
        lax.fori_loop(0, (15 + wide) // UNROLL[wide], add, 0)
        for block in range(first, first + wide):
            upright = yacc[(block - first) * LANES:(block - first + 1) * LANES].T
            if block < 8:
                now_ref[block * order:(block + 1) * order] = upright
            if block > 0:
                next_ref[(block - 1) * order:block * order] = upright

    @pl.when(jnp.logical_not(mine))
    def _():
        row_copy().wait_recv()
        sk_ref[0:order] = acc[4, :, 0:LANES]
        sk_ref[order:2 * order] = acc[4, :, LANES:2 * LANES]

    @pl.when(mine)
    def _():
        row_copy().wait_send()

    def sent(s, up, h):
        onward = (z < layers - 1) if up == 0 else (z > 0)

        @pl.when(onward)
        def _():
            along_z(s, 1 - up, h).wait_send()

        along_y(s, h).wait_send()
        sent_core(s, h)

    def sent_core(s, h):
        @pl.when(wanted(s, other))
        def _():
            to_core(s, h).wait_send()

    for h in (0, 1):
        along_y(r, h).wait_send()

        @pl.when(z > 0)
        def _(h=h):
            along_z(r, 0, h).wait_send()

        @pl.when(z < layers - 1)
        def _(h=h):
            along_z(r, 1, h).wait_send()

        sent_core(mate, h)
        for distance in (1, 2, 3):
            each_side(r, distance, lambda s, up, h=h: sent(s, up, h))
            each_side(mate, distance, lambda s, up, h=h: sent_core(s, h))
    swap(probe_part, 0).wait_send()

    @pl.when(c == 0)
    def _():
        swap(tail_part, 1).wait_send()

    swap(sketch_part, 2).wait_send()


def gathered_body(markov_head, markov_tail, probes):
    order = markov_head.shape[1]
    columns = probes.shape[1]
    anywhere = pl.BlockSpec(memory_space=pl.ANY)
    near = pl.BlockSpec(memory_space=pltpu.VMEM)
    dma = pltpu.SemaphoreType.DMA
    return pl.pallas_call(
        gathered_kernel,
        out_shape=(jax.ShapeDtypeStruct((2 * order, columns), jnp.float32),
                   jax.ShapeDtypeStruct((8 * order, columns), jnp.float32),
                   jax.ShapeDtypeStruct((8 * order, columns), jnp.float32)),
        in_specs=[anywhere] * 3,
        out_specs=(near, near, near),
        scratch_shapes=[
            pltpu.VMEM((32, 512, order), jnp.bfloat16),
            pltpu.VMEM((order, 24 * columns), jnp.bfloat16),
            pltpu.VMEM((24 * columns, order), jnp.bfloat16),
            pltpu.VMEM((5, order, 2 * columns), jnp.float32),
            pltpu.VMEM((5 * columns, order), jnp.float32),
            pltpu.VMEM((order, 2, order), jnp.bfloat16),
            pltpu.VMEM((order, 8, order), jnp.bfloat16),
            pltpu.VMEM((8 * order, columns), jnp.bfloat16),
            dma((3,)), dma((32,)), dma((16,)), dma((16,)), dma((16,)), dma((16,)), dma((4,)), dma((4,)),
        ],
        compiler_params=pltpu.CompilerParams(
            collective_id=0, has_side_effects=True, vmem_limit_bytes=56 * 1024 * 1024),
    )(markov_head.transpose(1, 0, 2), markov_tail.transpose(1, 0, 2), probes)


def solution(mesh):
    placed = (
        P(("cases", "row"), None, None),
        P(("cases", "col"), None, None),
        P(("cases", "col"), None),
    )
    fits = mesh.shape["row"] == 8 and mesh.shape["col"] == 2

    def parts(markov_head, markov_tail, probes):
        shapes = (markov_head.shape[0], markov_tail.shape[0], probes.shape[1])
        chosen = gathered_body if fits and shapes == (2, 8, LANES) else body
        return chosen(markov_head, markov_tail, probes)

    return jax.shard_map(
        parts,
        mesh=mesh,
        in_specs=placed,
        out_specs=(P(("cases", "row"), None), P(("cases", "col"), None), P(("cases", "col"), None)),
        check_vma=False,
    )
```
